256 devices in a mesh: seq: 64 (over z, x, y_hi), head: 4 (over y_lo, core).
Axes of the slice: x: 4, y: 4 (y_hi: 2, y_lo: 2; y = y_hi * 2 + y_lo), z: 8, core: 2. Of those that a mesh axis runs over, the one named last changes fastest.
Arguments:
- query_roll: bfloat16 [64, 480, 8192], P('seq', 'head'), may hold values from -100 to 100
- key_roll: bfloat16 [64, 480, 1024], P('seq', 'head'), may hold values from -6 to 6
- value_roll: bfloat16 [64, 480, 1024], P('seq', 'head'), may hold values from -6 to 6
- out_grad: bfloat16 [64, 480, 8192], P('seq', None, 'head'), may hold values from -96 to 96
- lengths: int32 [64], P('seq'), may hold values from 1 to 480, as said below
- visible: int32 [64, 4], P('seq'), may hold values 0 or 1
- key_prompt: bfloat16 [2048, 1024], P('seq', 'head'), may hold values from -4.5 to 4.5
- value_prompt: bfloat16 [2048, 1024], P('seq', 'head'), may hold values from -6 to 6
Outputs:
- attn_out: bfloat16 [64, 480, 8192], P('seq', None, 'head')
- query_grad: bfloat16 [64, 480, 8192], P('seq', 'head')
- key_grad: bfloat16 [64, 480, 1024], P('seq', 'head')
- value_grad: bfloat16 [64, 480, 1024], P('seq', 'head')
- prompt_key_grad: bfloat16 [2048, 1024], P('seq', 'head')
- prompt_value_grad: bfloat16 [2048, 1024], P('seq', 'head')
The draws below stay inside these ranges and needn't reach their ends.
Inputs may be any that keep to these rules, and one draw needn't show every extreme that they name: `lengths`: A rollout's live tokens are its first ones; some rollout has all 480 live.
All inputs are finite; a program needn't handle non-finite values. No bound on the sum of `visible` on one device may be relied on, other than what follows from the above.
Results may differ from the reference program's by a relative error of at most 0.02.
Values may be sent and summed in bfloat16 or wider, within the bound.
No kernel may reach another device: no remote copies, remote signals or barrier semaphores. Data moves between devices by JAX's collectives and lax.ppermute only.
A program may use at most 128 MiB of HBM per device.

```python
import jax
import jax.numpy as jnp
from jax import lax

HD = 128
GROUPS = 4
BLOCK = 128
RL = 480
P_DEV = 32
ROLLOUTS = 64
PROMPT = 512
PROMPT_ALL = 2048
PBLOCKS = 4
QF = 8192
KVF = 1024


def base_keys(key):
    return jnp.clip(jax.random.normal(key, (PROMPT_ALL, KVF), jnp.float32), -4.0, 4.0)


def draw_key_prompt(key, part):
    base_rows = base_keys(key)
    return base_rows.astype(jnp.bfloat16)


def draw_query_roll(key, part):
    key = jax.random.fold_in(key, 12)
    first_key = jax.random.fold_in(key, 0)
    queries = jnp.clip(jax.random.normal(first_key, (ROLLOUTS, RL, QF), jnp.float32), -4.0, 4.0)
    return queries.astype(jnp.bfloat16)


def draw_lengths(key, part):
    key = jax.random.fold_in(key, 13)
    first_key, second_key = jax.random.split(key)
    values_drawn = jax.random.randint(first_key, (ROLLOUTS,), 1, RL + 1, dtype=jnp.int32)
    chosen = jax.random.randint(second_key, (), 0, ROLLOUTS, dtype=jnp.int32)
    return jnp.where(jnp.arange(ROLLOUTS, dtype=jnp.int32) == chosen, RL, values_drawn).astype(jnp.int32)


def set_ends(drawn, rng, low, high):
    longest = drawn.shape.index(max(drawn.shape))
    spots = []
    for shift in (0, 1):
        where = [jax.random.randint(jax.random.fold_in(rng, axis), (), 0, length) for axis, length in enumerate(drawn.shape)]
        where[longest] = (where[longest] + shift) % drawn.shape[longest]
        spots.append(tuple(where))
    return drawn.at[spots[0]].set(low).at[spots[1]].set(high)


def block_scale(rng, shape, cuts, low, largest):
    factor_of = 1.0
    for position, parts in cuts:
        steps = jax.random.uniform(jax.random.fold_in(jax.random.fold_in(rng, 6), position), (parts,), jnp.float32, low / len(cuts), largest / len(cuts))
        factor_of = factor_of * jnp.repeat(jnp.exp(steps), shape[position] // parts).reshape((-1,) + (1,) * (len(shape) - 1 - position))
    return factor_of


def centred(key, extent, deviation, most, pieces=(), held_as=jnp.bfloat16):
    gain = block_scale(key, extent, pieces, -0.22, 0.18) if pieces else 1.0
    result = jax.random.normal(key, extent, jnp.float32) * deviation * gain
    return jnp.minimum(jnp.maximum(result, -most), most).astype(held_as)


def setup_inputs(seed: int = 0) -> dict:
    streams_of = jax.random.split(jax.random.key(seed), 9)
    query_roll = draw_query_roll(jax.random.fold_in(streams_of[8], 71), 0)
    key_roll = centred(streams_of[1], (ROLLOUTS, RL, KVF), 1.0, 6.0, ((0, 64), (1, 4)))
    value_roll = centred(streams_of[2], (ROLLOUTS, RL, KVF), 1.0, 6.0, ((0, 64), (1, 4)))
    out_grad = centred(streams_of[3], (ROLLOUTS, RL, QF), 16.0, 96.0, ((0, 64), (2, 4)))
    lengths = draw_lengths(jax.random.fold_in(streams_of[8], 71), 0)
    visible = set_ends((jax.random.randint(streams_of[5], (ROLLOUTS, PBLOCKS), 0, 2) < 1).astype(jnp.int32), jax.random.fold_in(streams_of[5], 1), 0, 1)
    key_prompt = draw_key_prompt(jax.random.fold_in(streams_of[8], 71), 0)
    value_prompt = centred(streams_of[7], (PROMPT_ALL, KVF), 1.0, 6.0, ((0, 64), (1, 4)))
    return {"query_roll": query_roll, "key_roll": key_roll, "value_roll": value_roll, "out_grad": out_grad, "lengths": lengths, "visible": visible, "key_prompt": key_prompt, "value_prompt": value_prompt}


masked_value = -1e30


def visibility(visible_row, length, row_count, prompt_rows):
    positions = jnp.arange(row_count, dtype=jnp.int32)
    prompt_ok = jnp.repeat(visible_row, BLOCK)[:prompt_rows] == 1
    own_ok = positions[None, :] <= positions[:, None]
    allowed = jnp.concatenate([jnp.broadcast_to(prompt_ok[None, :], (row_count, prompt_rows)), own_ok], axis=1)
    return allowed, positions < length


def attend(queries, keys_all, values_all, grad_out, allowed, live_rows):
    row_count = queries.shape[0]
    kv_heads = keys_all.shape[1] // HD
    scale_factor = HD ** -0.5
    query_four = queries.astype(jnp.float32).reshape(row_count, kv_heads, -1, HD)
    key_three = keys_all.astype(jnp.float32).reshape(-1, kv_heads, HD)
    value_three = values_all.astype(jnp.float32).reshape(-1, kv_heads, HD)
    live_mask = live_rows[:, None, None, None]
    grad_four = jnp.where(live_mask, grad_out.reshape(row_count, kv_heads, -1, HD), jnp.zeros((), grad_out.dtype)).astype(jnp.float32)
    scores = jnp.einsum("tgjd,kgd->gjtk", query_four, key_three) * scale_factor
    scores = jnp.where(allowed[None, None], scores, masked_value)
    shifted = jnp.exp(scores - jnp.max(scores, axis=-1, keepdims=True))
    weights = shifted / jnp.sum(shifted, axis=-1, keepdims=True)
    weights_low = lax.optimization_barrier(weights.astype(jnp.bfloat16)).astype(jnp.float32)
    mixed = jnp.einsum("gjtk,kgd->tgjd", weights_low, value_three)
    attn_out = jnp.where(live_mask, mixed, 0.0).astype(jnp.bfloat16).reshape(row_count, -1)
    delta = jnp.sum(grad_four * mixed, axis=-1)
    dprob = jnp.einsum("tgjd,kgd->gjtk", grad_four, value_three)
    dscore = weights * (dprob - jnp.transpose(delta, (1, 2, 0))[..., None])
    dscore_low = lax.optimization_barrier(dscore.astype(jnp.bfloat16)).astype(jnp.float32)
    query_grad = (jnp.einsum("gjtk,kgd->tgjd", dscore_low, key_three) * scale_factor).astype(jnp.bfloat16).reshape(row_count, -1)
    key_grad = (jnp.einsum("gjtk,tgjd->kgd", dscore_low, query_four) * scale_factor).reshape(-1, kv_heads * HD)
    value_grad = jnp.einsum("gjtk,tgjd->kgd", weights_low, grad_four).reshape(-1, kv_heads * HD)
    return attn_out, query_grad, key_grad, value_grad


def reference(query_roll, key_roll, value_roll, out_grad, lengths, visible, key_prompt, value_prompt):
    per_group = ROLLOUTS // GROUPS

    def group_stack(array):
        return jnp.swapaxes(array.reshape((per_group, GROUPS) + array.shape[1:]), 0, 1)

    def group_unstack(array):
        return jnp.swapaxes(array, 0, 1).reshape((ROLLOUTS,) + array.shape[2:])

    def prompt_stack(array):
        return jnp.transpose(array.reshape(per_group, GROUPS, P_DEV, KVF), (1, 0, 2, 3)).reshape(GROUPS, PROMPT, KVF)

    def prompt_unstack(array):
        return jnp.transpose(array.reshape(GROUPS, per_group, P_DEV, KVF), (1, 0, 2, 3)).reshape(PROMPT_ALL, KVF)

    def run_group(group_inputs):
        queries, keys_own, values_own, grads, lengths_group, visible_group, keys_prompt, values_prompt = group_inputs

        def per_rollout(totals, rollout_inputs):
            query_now, key_now, value_now, grad_now, length_now, visible_now = rollout_inputs
            allowed, live_rows = visibility(visible_now, length_now, RL, PROMPT)
            attn_out, query_grad, key_grad, value_grad = attend(
                query_now,
                jnp.concatenate([keys_prompt, key_now], axis=0),
                jnp.concatenate([values_prompt, value_now], axis=0),
                grad_now, allowed, live_rows)
            totals = (totals[0] + key_grad[:PROMPT], totals[1] + value_grad[:PROMPT])
            return totals, (attn_out, query_grad, key_grad[PROMPT:].astype(jnp.bfloat16), value_grad[PROMPT:].astype(jnp.bfloat16))

        zeros_start = jnp.zeros((PROMPT, KVF), jnp.float32)
        totals, outputs = lax.scan(per_rollout, (zeros_start, zeros_start),
                                   (queries, keys_own, values_own, grads, lengths_group, visible_group))
        return outputs + (totals[0].astype(jnp.bfloat16), totals[1].astype(jnp.bfloat16))

    results = lax.map(run_group, (
        group_stack(query_roll), group_stack(key_roll), group_stack(value_roll), group_stack(out_grad),
        group_stack(lengths), group_stack(visible),
        prompt_stack(key_prompt), prompt_stack(value_prompt)))
    attn_out = group_unstack(results[0])
    query_grad = group_unstack(results[1])
    key_grad = group_unstack(results[2])
    value_grad = group_unstack(results[3])
    prompt_key_grad = prompt_unstack(results[4])
    prompt_value_grad = prompt_unstack(results[5])
    return (attn_out, query_grad, key_grad, value_grad, prompt_key_grad, prompt_value_grad)
```

```python
import functools

import jax
import jax.numpy as jnp
from jax import lax
from jax.experimental import pallas as pl
from jax.experimental.pallas import tpu as pltpu
from jax.sharding import PartitionSpec as P

HD = 128
BLOCK = 128
GROUPS = 4
SCALE = HD ** (-0.5)
EXP_SCALE = SCALE * 1.4426950408889634
MASKED = -1e30
VMEM_BYTES = 48 * 1024 * 1024
SMEM = pl.BlockSpec(memory_space=pltpu.SMEM)
VMEM = pl.BlockSpec(memory_space=pltpu.VMEM)
HBM = pl.BlockSpec(memory_space=pl.ANY)
PARAMS = pltpu.CompilerParams(vmem_limit_bytes=VMEM_BYTES)


def dot_nt(left, right):
    return lax.dot_general(left, right, (((1,), (1,)), ((), ())), preferred_element_type=jnp.float32)


def dot_nn(left, right):
    return jnp.dot(left, right, preferred_element_type=jnp.float32)


def here():
    rank = lax.axis_index("seq") // GROUPS
    return lax.axis_index("head"), rank // 4, rank % 4


def prep_kernel(rows, visible_ref, p0, p1, p2, p3, own0, own1, own2, own3, kc, vc, kct, vct, own_rows, block_rows):
    me, high, low = here()
    own_rows[4 * rows :, :] = jnp.zeros((4 * BLOCK - 4 * rows, 4 * HD), jnp.float32)
    for k, ref in enumerate((own0, own1, own2, own3)):
        start = pl.multiple_of((me ^ k) * rows, 8)
        own_rows[pl.ds(start, rows), :] = ref[...].astype(jnp.float32)
    targets = ((kc, kct, 0), (kc, kct, 1), (vc, vct, 0), (vc, vct, 1))

    def place(slot, block):
        at = pl.multiple_of(slot * BLOCK, BLOCK)
        for part, (plain, turned, g) in enumerate(targets):
            piece = block[:, part * HD : (part + 1) * HD]
            plain[g, pl.ds(at, BLOCK), :] = piece.astype(jnp.bfloat16)
            turned[g, :, pl.ds(at, BLOCK)] = piece.T.astype(jnp.bfloat16)

    slot = jnp.int32(0)
    for b in range(4):
        seen = visible_ref[0, b]

        @pl.when(seen == 1)
        def _(b=b, slot=slot):
            for j, ref in enumerate((p0, p1, p2, p3)):
                start = pl.multiple_of((low ^ j) * 32, 32)
                block_rows[pl.ds(start, 32), :] = ref[high ^ b].astype(jnp.float32)
            place(slot, block_rows[...])

        slot = slot + seen
    for b in range(4):
        place(slot + b, own_rows[b * BLOCK : (b + 1) * BLOCK, :])


def prep(visible, prompts, owns):
    rows = owns[0].shape[0]
    shapes = [(2, 8 * BLOCK, HD)] * 2 + [(2, HD, 8 * BLOCK)] * 2
    return pl.pallas_call(
        functools.partial(prep_kernel, rows),
        out_shape=[jax.ShapeDtypeStruct(shape, jnp.bfloat16) for shape in shapes],
        in_specs=[SMEM] + [VMEM] * 8,
        out_specs=[VMEM] * 4,
        scratch_shapes=[pltpu.VMEM((4 * BLOCK, 4 * HD), jnp.float32), pltpu.VMEM((BLOCK, 4 * HD), jnp.float32)],
        compiler_params=PARAMS,
        name="prep",
    )(visible, *prompts, *owns)


def unit(n, heads, rows, position, live, i, q_ref, g_ref, kc, vc, kct, vct, out_ref, qg_ref, dk_ref, dv_ref):
    keys = n * BLOCK
    width = heads * BLOCK
    kv = i // (8 // heads)
    pad = jnp.zeros((BLOCK - rows, HD), jnp.float32)
    row_live = lax.broadcasted_iota(jnp.int32, (rows, HD), 0) < live

    def at(h):
        return pl.ds(pl.multiple_of((i * heads + h) * HD, HD), HD)

    def turned(load, keep):
        parts = []
        for h in range(heads):
            x = load(h).astype(jnp.float32)
            if keep is not None:
                x = jnp.where(keep, x, 0.0)
            parts.append(jnp.concatenate([x, pad], axis=0).T)
        return jnp.concatenate(parts, axis=1)

    q_t = turned(lambda h: q_ref[:, at(h)], None)
    g_t = turned(lambda h: g_ref[position, :, at(h)], row_live)
    q_low = q_t.astype(jnp.bfloat16)
    g_low = g_t.astype(jnp.bfloat16)
    scores = dot_nn(kc[kv, :keys, :], q_low)
    masked_blocks = min(2, n)
    first = keys - masked_blocks * BLOCK
    shape = (BLOCK, width)
    s_at = lax.broadcasted_iota(jnp.int32, shape, 0)
    t_at = position * rows + lax.broadcasted_iota(jnp.int32, shape, 1) % BLOCK
    pieces = [scores[:first]] if first else []
    for j in range(masked_blocks):
        own = position - masked_blocks + 1 + j
        base = jnp.where(own >= 0, own * BLOCK, -100000)
        part = scores[first + j * BLOCK : first + (j + 1) * BLOCK]
        pieces.append(jnp.where(s_at + base <= t_at, part, MASKED))
    scores = jnp.concatenate(pieces, axis=0)
    top = jnp.max(scores, axis=0, keepdims=True)
    weights = jnp.exp2((scores - top) * EXP_SCALE)
    inverse = 1.0 / jnp.sum(weights, axis=0, keepdims=True)
    weights_low = weights.astype(jnp.bfloat16)
    mixed = dot_nn(vct[kv, :, :keys], weights_low) * inverse
    delta = jnp.sum(g_t * mixed, axis=0, keepdims=True)
    dprob = dot_nn(vc[kv, :keys, :], g_low)
    dscore = (weights * (dprob - delta)).astype(jnp.bfloat16)
    inverse_scaled = inverse * SCALE
    query_grad = dot_nn(kct[kv, :, :keys], dscore) * inverse_scaled
    g_scaled = (g_t * inverse).astype(jnp.bfloat16)
    q_scaled = (q_t * inverse_scaled).astype(jnp.bfloat16)
    dv_ref[kv, :keys, :] += dot_nt(weights_low, g_scaled)
    dk_ref[kv, :keys, :] += dot_nt(dscore, q_scaled)
    for h in range(heads):
        lanes = slice(h * BLOCK, (h + 1) * BLOCK)
        mixed_rows = mixed[:, lanes].T[:rows]
        out_ref[:, at(h)] = jnp.where(row_live, mixed_rows, 0.0).astype(jnp.bfloat16)
        qg_ref[:, at(h)] = query_grad[:, lanes].T[:rows].astype(jnp.bfloat16)


def main_kernel(k, heads, rows, visible_ref, length_ref, q_ref, g_ref, kc, vc, kct, vct, *rest):
    if k == 0:
        attn, qg_out, dk_ref, dv_ref, out_ref, qg_ref, sems = rest
        dk_ref[...] = jnp.zeros_like(dk_ref)
        dv_ref[...] = jnp.zeros_like(dv_ref)
    else:
        _, _, _, attn, qg_ref, dk_ref, dv_ref, out_ref, sems = rest
    me = lax.axis_index("head")
    position = me ^ k
    seen = visible_ref[0, 0] + visible_ref[0, 1] + visible_ref[0, 2] + visible_ref[0, 3]
    live = length_ref[0] - position * rows
    total_heads = q_ref.shape[1] // HD

    @pl.when(live <= 0)
    def _():
        out_ref[...] = jnp.zeros_like(out_ref)
        qg_ref[...] = jnp.zeros_like(qg_ref)

    count = jnp.where(live > 0, seen + position + 1, 0)
    for n in range(1, 9):

        @pl.when(count == n)
        def _(n=n):
            @pl.loop(0, total_heads // heads)
            def _(i):
                unit(n, heads, rows, position, live, i, q_ref, g_ref, kc, vc, kct, vct, out_ref, qg_ref, dk_ref, dv_ref)

    copies = [pltpu.make_async_copy(out_ref, attn.at[position], sems.at[0])]
    if k == 0:
        cols = q_ref.shape[1]
        target = qg_out.at[:, pl.ds(pl.multiple_of(me * cols, cols), cols)]
        copies.append(pltpu.make_async_copy(qg_ref, target, sems.at[1]))
    for copy in copies:
        copy.start()
    for copy in copies:
        copy.wait()


def main(k, visible, lengths, q, grad, caches, carried, heads=4):
    rows, cols = q.shape
    total = jax.ShapeDtypeStruct((2, 8 * BLOCK, HD), jnp.float32)
    small = jax.ShapeDtypeStruct((rows, cols), jnp.bfloat16)
    wide = jax.ShapeDtypeStruct((rows, 4 * cols), jnp.bfloat16)
    attn = jax.ShapeDtypeStruct(grad.shape, jnp.bfloat16)
    buffer = pltpu.VMEM((rows, cols), jnp.bfloat16)
    in_specs = [SMEM] * 2 + [VMEM] * 6
    args = [visible, lengths, q, grad, *caches]
    aliases = {}
    if k:
        aliases = {8: 0, 9: 2, 10: 3}
        in_specs += [HBM, VMEM, VMEM]
        args += list(carried)
    flops = 6 * 2 * 16 * rows * 800 * HD
    return pl.pallas_call(
        functools.partial(main_kernel, k, heads, rows),
        out_shape=[attn, small if k else wide, total, total],
        in_specs=in_specs,
        out_specs=[HBM, VMEM if k else HBM, VMEM, VMEM],
        scratch_shapes=[buffer] * (1 if k else 2) + [pltpu.SemaphoreType.DMA((2,))],
        input_output_aliases=aliases,
        compiler_params=PARAMS,
        cost_estimate=pl.CostEstimate(flops=flops, bytes_accessed=6000000, transcendentals=0),
        name="rows_%d" % k,
    )(*args)


def finish_kernel(rows, visible_ref, dk_ref, dv_ref, *outs):
    me, high, low = here()
    pieces, owns = outs[:4], outs[4:]
    parts = ((dk_ref, 0), (dk_ref, 1), (dv_ref, 0), (dv_ref, 1))
    slot = jnp.int32(0)
    for b in range(4):
        seen = visible_ref[0, b]

        @pl.when(seen == 1)
        def _(b=b, slot=slot):
            for j, piece in enumerate(pieces):
                source = pl.ds(pl.multiple_of(slot * BLOCK + (low ^ j) * 32, 32), 32)
                for part, (ref, g) in enumerate(parts):
                    piece[b, :, part * HD : (part + 1) * HD] = ref[g, source, :].astype(piece.dtype)

        @pl.when(seen != 1)
        def _(b=b):
            for piece in pieces:
                piece[b] = jnp.zeros(piece.shape[1:], piece.dtype)

        slot = slot + seen
    for k, own in enumerate(owns):
        source = pl.ds(pl.multiple_of(slot * BLOCK + (me ^ k) * rows, 8), rows)
        for part, (ref, g) in enumerate(parts):
            own[:, part * HD : (part + 1) * HD] = ref[g, source, :].astype(own.dtype)


def finish(visible, sums, rows):
    shapes = [jax.ShapeDtypeStruct((4, 32, 4 * HD), jnp.float32 if j == 0 else jnp.bfloat16) for j in range(4)]
    return pl.pallas_call(
        functools.partial(finish_kernel, rows),
        out_shape=shapes + [jax.ShapeDtypeStruct((rows, 4 * HD), jnp.bfloat16)] * 4,
        in_specs=[SMEM] + [VMEM] * 2,
        out_specs=[VMEM] * 8,
        compiler_params=PARAMS,
        name="finish",
    )(visible, *sums)


def partner(value, mask, axis="head"):
    pairs = [(source, source ^ mask) for source in range(lax.axis_size(axis))]
    return lax.ppermute(value, axis, pairs)


def after(value, *earlier):
    return lax.optimization_barrier((value, *earlier))[0]


def per_device(query_roll, key_roll, value_roll, out_grad, lengths, visible, key_prompt, value_prompt):
    rows = query_roll.shape[1]
    me, high, low = here()
    queries, keys, values = query_roll[0], key_roll[0], value_roll[0]
    q_cols = queries.shape[1] // 4
    kv_cols = keys.shape[1] // 4

    def columns(array, index, size):
        return lax.dynamic_slice_in_dim(array, index * size, size, 1)

    def kv_piece(index):
        return jnp.concatenate([columns(keys, index, kv_cols), columns(values, index, kv_cols)], axis=1)

    with jax.named_scope("gather_prompt_far"):
        mine = jnp.concatenate([key_prompt, value_prompt], axis=1)
        four = jnp.stack([mine] + [partner(mine, 16 * j, "seq") for j in (1, 2, 3)])
    with jax.named_scope("send_kv"):
        owns = [kv_piece(me)] + [partner(kv_piece(me ^ k), k) for k in (1, 2, 3)]
    with jax.named_scope("gather_prompt_near"):
        prompts = [four] + [partner(four, 4 * j, "seq") for j in (1, 2, 3)]
    with jax.named_scope("send_queries"):
        received = {0: columns(queries, me, q_cols)}
        received[2] = partner(after(columns(queries, me ^ 2, q_cols), *owns), 2)
        received[1] = partner(after(columns(queries, me ^ 1, q_cols), *owns), 1)
    caches = prep(visible, prompts, owns)
    grads = out_grad.reshape(4, rows, out_grad.shape[2])
    attn, query_grad, *sums = main(0, visible, lengths, received[0], grads, caches, None)
    with jax.named_scope("send_queries"):
        received[3] = partner(after(columns(queries, me ^ 3, q_cols), received[2]), 3)
    back = {}
    for k in (2, 1, 3):
        attn, part, *sums = main(k, visible, lengths, received[k], grads, caches, (attn, *sums))
        with jax.named_scope("return_query_grads"):
            back[k] = partner(part, k)
    near0, near1, near2, near3, *own_grads = finish(visible, sums, rows)
    with jax.named_scope("sum_prompt_grads_near"):
        near = [near0] + [partner(piece, 4 * j, "seq") for j, piece in ((1, near1), (2, near2), (3, near3))]
        partial = sum(piece.astype(jnp.float32) for piece in near)
    with jax.named_scope("sum_prompt_grads_far"):
        def block(index):
            return lax.dynamic_index_in_dim(partial, index, 0, keepdims=False)

        far = [block(high)] + [partner(block(high ^ j).astype(jnp.bfloat16), 16 * j, "seq") for j in (1, 2, 3)]
        summed = sum(piece.astype(jnp.float32) for piece in far).astype(jnp.bfloat16)
    with jax.named_scope("return_kv_grads"):
        kv_back = [own_grads[0]] + [partner(own_grads[k], k) for k in (1, 2, 3)]
    for k in (2, 1, 3):
        query_grad = lax.dynamic_update_slice_in_dim(query_grad, back[k], (me ^ k) * q_cols, 1)
    key_grad = jnp.zeros_like(keys)
    value_grad = jnp.zeros_like(values)
    for k in range(4):
        key_grad = lax.dynamic_update_slice_in_dim(key_grad, kv_back[k][:, :kv_cols], (me ^ k) * kv_cols, 1)
        value_grad = lax.dynamic_update_slice_in_dim(value_grad, kv_back[k][:, kv_cols:], (me ^ k) * kv_cols, 1)
    return (
        attn.reshape(1, 4 * rows, q_cols),
        query_grad[None],
        key_grad[None],
        value_grad[None],
        summed[:, :kv_cols],
        summed[:, kv_cols:],
    )


def solution(mesh):
    in_specs = (
        P("seq", "head", None),
        P("seq", "head", None),
        P("seq", "head", None),
        P("seq", None, "head"),
        P("seq"),
        P("seq", None),
        P("seq", "head"),
        P("seq", "head"),
    )
    out_specs = (
        P("seq", None, "head"),
        P("seq", "head", None),
        P("seq", "head", None),
        P("seq", "head", None),
        P("seq", "head"),
        P("seq", "head"),
    )
    return jax.shard_map(per_device, mesh=mesh, in_specs=in_specs, out_specs=out_specs, check_vma=False)
```

```python
import functools

import jax
import jax.numpy as jnp
from jax import lax
from jax.experimental import pallas as pl
from jax.experimental.pallas import tpu as pltpu
from jax.sharding import PartitionSpec as P

HD = 128
BLOCK = 128
GROUPS = 4
SCALE = HD ** (-0.5)
EXP_SCALE = SCALE * 1.4426950408889634
MASKED = -1e30
LAST = 1
VMEM_BYTES = 28 * 1024 * 1024
SMEM = pl.BlockSpec(memory_space=pltpu.SMEM)
VMEM = pl.BlockSpec(memory_space=pltpu.VMEM)
HBM = pl.BlockSpec(memory_space=pl.ANY)
PARAMS = pltpu.CompilerParams(vmem_limit_bytes=VMEM_BYTES)


def dot_nt(left, right):
    return lax.dot_general(left, right, (((1,), (1,)), ((), ())), preferred_element_type=jnp.float32)


def dot_nn(left, right):
    return jnp.dot(left, right, preferred_element_type=jnp.float32)


def here():
    rank = lax.axis_index("seq") // GROUPS
    return lax.axis_index("head"), rank // 4, rank % 4


def prep_kernel(rows, visible_ref, p0, p1, p2, p3, own0, own1, own2, own3, kc, vc, kct, vct, own_rows, block_rows):
    me, high, low = here()
    own_rows[4 * rows :, :] = jnp.zeros((4 * BLOCK - 4 * rows, 4 * HD), jnp.float32)
    for k, ref in enumerate((own0, own1, own2, own3)):
        start = pl.multiple_of((me ^ k) * rows, 8)
        own_rows[pl.ds(start, rows), :] = ref[...].astype(jnp.float32)
    targets = ((kc, kct, 0), (kc, kct, 1), (vc, vct, 0), (vc, vct, 1))

    def place(slot, block):
        at = pl.multiple_of(slot * BLOCK, BLOCK)
        for part, (plain, turned, g) in enumerate(targets):
            piece = block[:, part * HD : (part + 1) * HD]
            plain[g, pl.ds(at, BLOCK), :] = piece.astype(jnp.bfloat16)
            turned[g, :, pl.ds(at, BLOCK)] = piece.T.astype(jnp.bfloat16)

    slot = jnp.int32(0)
    for b in range(4):
        seen = visible_ref[0, b]

        @pl.when(seen == 1)
        def _(b=b, slot=slot):
            for j, ref in enumerate((p0, p1, p2, p3)):
                start = pl.multiple_of((low ^ j) * 32, 32)
                block_rows[pl.ds(start, 32), :] = ref[high ^ b].astype(jnp.float32)
            place(slot, block_rows[...])

        slot = slot + seen
    for b in range(4):
        place(slot + b, own_rows[b * BLOCK : (b + 1) * BLOCK, :])

    @pl.when(slot < 4)
    def _():
        place(slot + 4, jnp.zeros((BLOCK, 4 * HD), jnp.float32))


def prep(visible, prompts, owns):
    rows = owns[0].shape[0]
    shapes = [(2, 8 * BLOCK, HD)] * 2 + [(2, HD, 8 * BLOCK)] * 2
    return pl.pallas_call(
        functools.partial(prep_kernel, rows),
        out_shape=[jax.ShapeDtypeStruct(shape, jnp.bfloat16) for shape in shapes],
        in_specs=[SMEM] + [VMEM] * 8,
        out_specs=[VMEM] * 4,
        scratch_shapes=[pltpu.VMEM((4 * BLOCK, 4 * HD), jnp.float32), pltpu.VMEM((BLOCK, 4 * HD), jnp.float32)],
        compiler_params=PARAMS,
        name="prep",
    )(visible, *prompts, *owns)


def unit(n, heads, rows, position, seen, live, i, q_ref, g_ref, kc, vc, kct, vct, out_ref, qg_ref, dk_ref, dv_ref):
    keys = n * BLOCK
    width = heads * BLOCK
    kv = i // (8 // heads)
    pad = jnp.zeros((BLOCK - rows, HD), jnp.float32)
    row_live = lax.broadcasted_iota(jnp.int32, (rows, HD), 0) < live

    def at(h):
        return pl.ds(pl.multiple_of((i * heads + h) * HD, HD), HD)

    def padded(x):
        return jnp.concatenate([x, pad], axis=0).astype(jnp.bfloat16)

    q_low = jnp.concatenate([padded(q_ref[:, at(h)].astype(jnp.float32)) for h in range(heads)], axis=0)
    g_low = jnp.concatenate(
        [padded(jnp.where(row_live, g_ref[:, at(h)].astype(jnp.float32), 0.0)) for h in range(heads)], axis=0
    )
    scores = dot_nt(kc[kv, :keys, :], q_low)
    masked_blocks = min(3, n)
    first = keys - masked_blocks * BLOCK
    last = n - 1 - seen
    shape = (BLOCK, width)
    s_at = lax.broadcasted_iota(jnp.int32, shape, 0)
    t_at = position * rows + lax.broadcasted_iota(jnp.int32, shape, 1) % BLOCK
    pieces = [scores[:first]] if first else []
    for j in range(masked_blocks):
        own = last - masked_blocks + 1 + j
        base = jnp.where(own >= 0, own * BLOCK, -100000)
        part = scores[first + j * BLOCK : first + (j + 1) * BLOCK]
        pieces.append(jnp.where(s_at + base <= t_at, part, MASKED))
    scores = jnp.concatenate(pieces, axis=0)
    top = jnp.max(scores, axis=0, keepdims=True)
    weights = jnp.exp2((scores - top) * EXP_SCALE)
    weights = weights * (1.0 / jnp.sum(weights, axis=0, keepdims=True))
    weights_low = weights.astype(jnp.bfloat16)
    dprob = dot_nt(vc[kv, :keys, :], g_low)
    product = weights * dprob
    delta = jnp.sum(product, axis=0, keepdims=True)
    dscore = (product - weights * delta).astype(jnp.bfloat16)
    mixed = dot_nn(vct[kv, :, :keys], weights_low).astype(jnp.bfloat16)
    query_grad = (dot_nn(kct[kv, :, :keys], dscore) * SCALE).astype(jnp.bfloat16)
    dv_ref[kv, :keys, :] += dot_nn(weights_low, g_low)
    dk_ref[kv, :keys, :] += dot_nn(dscore, q_low)
    for h in range(heads):
        lanes = slice(h * BLOCK, (h + 1) * BLOCK)
        mixed_rows = mixed[:, lanes].T.astype(jnp.float32)[:rows]
        out_ref[:, at(h)] = jnp.where(row_live, mixed_rows, 0.0).astype(jnp.bfloat16)
        qg_ref[:, at(h)] = query_grad[:, lanes].T[:rows]


def finish(rows, visible_ref, dk_ref, dv_ref, pieces, owns):
    me, _, low = here()
    parts = ((dk_ref, 0, SCALE), (dk_ref, 1, SCALE), (dv_ref, 0, 1.0), (dv_ref, 1, 1.0))
    slot = jnp.int32(0)
    for b in range(4):
        seen = visible_ref[0, b]

        @pl.when(seen == 1)
        def _(b=b, slot=slot):
            for j, piece in enumerate(pieces):
                source = pl.ds(pl.multiple_of(slot * BLOCK + (low ^ j) * 32, 32), 32)
                for part, (ref, g, scale) in enumerate(parts):
                    piece[b, :, part * HD : (part + 1) * HD] = (ref[g, source, :] * scale).astype(piece.dtype)

        @pl.when(seen != 1)
        def _(b=b):
            for piece in pieces:
                piece[b] = jnp.zeros(piece.shape[1:], piece.dtype)

        slot = slot + seen
    for k, own in enumerate(owns):
        source = pl.ds(pl.multiple_of(slot * BLOCK + (me ^ k) * rows, 8), rows)
        for part, (ref, g, scale) in enumerate(parts):
            own[:, own.shape[1] - (4 - part) * HD : own.shape[1] - (3 - part) * HD] = (ref[g, source, :] * scale).astype(own.dtype)


def main_kernel(k, heads, rows, visible_ref, length_ref, q_ref, kc, vc, kct, vct, grads, *rest):
    if k == 0:
        attn, wide, dk_ref, dv_ref, g_ref, out_ref, sems, qg_ref = rest
        dk_ref[...] = jnp.zeros_like(dk_ref)
        dv_ref[...] = jnp.zeros_like(dv_ref)
    else:
        _, _, _, attn, qg_ref, dk_ref, dv_ref, *finals, g_ref, out_ref, sems = rest
    me = lax.axis_index("head")
    position = me ^ k
    seen = visible_ref[0, 0] + visible_ref[0, 1] + visible_ref[0, 2] + visible_ref[0, 3]
    live = length_ref[0] - position * rows
    cols = q_ref.shape[1]
    size = heads * HD
    steps = cols // size

    def chunk(i):
        return pl.ds(pl.multiple_of(i * size, size), size)

    def grad_copy(i):
        return pltpu.make_async_copy(grads.at[position, :, chunk(i)], g_ref.at[:, chunk(i)], sems.at[0, i])

    def out_copies(i):
        copies = [pltpu.make_async_copy(out_ref.at[:, chunk(i)], attn.at[position, :, chunk(i)], sems.at[1, i])]
        if k == 0:
            target = wide.at[:, pl.ds(pl.multiple_of(me * cols + i * size, size), size)]
            copies.append(pltpu.make_async_copy(qg_ref.at[:, chunk(i)], target, sems.at[2, i]))
        return copies

    def send(i):
        for copy in out_copies(i):
            copy.start()

    @pl.when(live <= 0)
    def _():
        out_ref[...] = jnp.zeros_like(out_ref)
        qg_ref[:, :cols] = jnp.zeros((rows, cols), jnp.bfloat16)
        for i in range(steps):
            send(i)

    @pl.when(live > 0)
    def _():
        for i in range(steps):
            grad_copy(i).start()

    count = jnp.where(live > 0, (seen + position + 2) // 2 * 2, 0)
    for n in (2, 4, 6, 8):

        @pl.when(count == n)
        def _(n=n):
            @pl.loop(0, steps)
            def _(i):
                grad_copy(i).wait()
                unit(n, heads, rows, position, seen, live, i, q_ref, g_ref, kc, vc, kct, vct, out_ref, qg_ref, dk_ref, dv_ref)
                send(i)

    if k == LAST:
        finish(rows, visible_ref, dk_ref, dv_ref, finals[:4], [finals[4], qg_ref, finals[5], finals[6]])
    for i in range(steps):
        for copy in out_copies(i):
            copy.wait()


def main(k, visible, lengths, q, grad, caches, carried, heads=4):
    rows, cols = q.shape
    total = jax.ShapeDtypeStruct((2, 8 * BLOCK, HD), jnp.float32)
    small = jax.ShapeDtypeStruct((rows, cols), jnp.bfloat16)
    wide = jax.ShapeDtypeStruct((rows, 4 * cols), jnp.bfloat16)
    attn = jax.ShapeDtypeStruct(grad.shape, jnp.bfloat16)
    buffer = pltpu.VMEM((rows, cols), jnp.bfloat16)
    first = k == 0
    finals = []
    if k == LAST:
        kv = 4 * HD
        small = jax.ShapeDtypeStruct((rows, cols + kv), jnp.bfloat16)
        finals = [jax.ShapeDtypeStruct((4, 32, kv), jnp.bfloat16 if j else jnp.float32) for j in range(4)]
        finals += [jax.ShapeDtypeStruct((rows, kv), jnp.bfloat16)] * 3
    flops = 6 * 2 * 16 * rows * 800 * HD
    return pl.pallas_call(
        functools.partial(main_kernel, k, heads, rows),
        out_shape=[attn, wide if first else small, total, total] + finals,
        in_specs=[SMEM] * 2 + [VMEM] * 5 + [HBM] + ([] if first else [HBM, VMEM, VMEM]),
        out_specs=[HBM, HBM if first else VMEM, VMEM, VMEM] + [VMEM] * len(finals),
        scratch_shapes=[buffer] * 2 + [pltpu.SemaphoreType.DMA((3, cols // (heads * HD)))] + [buffer] * first,
        input_output_aliases={} if first else {8: 0, 9: 2, 10: 3},
        compiler_params=PARAMS,
        cost_estimate=pl.CostEstimate(flops=flops, bytes_accessed=6000000, transcendentals=0),
        name="rows_%d" % k,
    )(visible, lengths, q, *caches, grad, *([] if first else carried))


def assemble_kernel(k, piece_ref, _, wide, sem):
    cols = wide.shape[1] // 4
    start = pl.multiple_of((lax.axis_index("head") ^ k) * cols, cols)
    copy = pltpu.make_async_copy(piece_ref.at[:, :cols], wide.at[:, pl.ds(start, cols)], sem)
    copy.start()
    copy.wait()


def assemble(k, piece, wide):
    return pl.pallas_call(
        functools.partial(assemble_kernel, k),
        out_shape=jax.ShapeDtypeStruct(wide.shape, wide.dtype),
        in_specs=[VMEM, HBM],
        out_specs=HBM,
        scratch_shapes=[pltpu.SemaphoreType.DMA],
        input_output_aliases={1: 0},
        name="assemble",
    )(piece, wide)


def assemble_kv_kernel(p0, p1, p2, p3, key_grad, value_grad, sems):
    me = lax.axis_index("head")
    cols = p0.shape[1] // 2
    copies = []
    for k, piece in enumerate((p0, p1, p2, p3)):
        at = pl.ds(pl.multiple_of((me ^ k) * cols, cols), cols)
        offset = piece.shape[1] - 2 * cols
        for j, target in enumerate((key_grad, value_grad)):
            source = piece.at[:, offset + j * cols : offset + (j + 1) * cols]
            copies.append(pltpu.make_async_copy(source, target.at[:, at], sems.at[j, k]))
    for copy in copies:
        copy.start()
    for copy in copies:
        copy.wait()


def assemble_kv(pieces):
    rows, cols = pieces[0].shape
    shape = jax.ShapeDtypeStruct((rows, 2 * cols), pieces[0].dtype)
    return pl.pallas_call(
        assemble_kv_kernel,
        out_shape=[shape, shape],
        in_specs=[VMEM] * 4,
        out_specs=[HBM] * 2,
        scratch_shapes=[pltpu.SemaphoreType.DMA((2, 4))],
        name="assemble_kv",
    )(*pieces)


def partner(value, mask, axis="head"):
    pairs = [(source, source ^ mask) for source in range(lax.axis_size(axis))]
    return lax.ppermute(value, axis, pairs)


def after(value, *earlier):
    return lax.optimization_barrier((value, *earlier))[0]


def per_device(query_roll, key_roll, value_roll, out_grad, lengths, visible, key_prompt, value_prompt):
    rows = query_roll.shape[1]
    me, high, low = here()
    queries, keys, values = query_roll[0], key_roll[0], value_roll[0]
    q_cols = queries.shape[1] // 4
    kv_cols = keys.shape[1] // 4

    def columns(array, index, size):
        return lax.dynamic_slice_in_dim(array, index * size, size, 1)

    def kv_piece(index):
        return jnp.concatenate([columns(keys, index, kv_cols), columns(values, index, kv_cols)], axis=1)

    with jax.named_scope("gather_prompt_far"):
        mine = jnp.concatenate([key_prompt, value_prompt], axis=1)
        four = jnp.stack([mine] + [partner(mine, 16 * j, "seq") for j in (1, 2, 3)])
    with jax.named_scope("gather_prompt_near"):
        prompts = [four] + [partner(four, 4 * j, "seq") for j in (1, 2, 3)]
    with jax.named_scope("send_kv"):
        owns = [kv_piece(me), None] + [partner(kv_piece(me ^ k), k) for k in (2, 3)]
        owns[1] = partner(after(kv_piece(me ^ 1), prompts[1]), 1)
    caches = prep(visible, prompts, owns)
    grads = out_grad.reshape(4, rows, out_grad.shape[2])
    q_pieces = [columns(queries, me ^ k, q_cols) for k in range(4)]
    with jax.named_scope("send_queries"):
        early = after([q_pieces[1], q_pieces[2]], *prompts)
        received = {k: partner(early[k - 1], k) for k in (1, 2)}
    attn, query_grad, *sums = main(0, visible, lengths, q_pieces[0], grads, caches, None)
    with jax.named_scope("send_queries"):
        received[3] = partner(after(q_pieces[3], sums[0]), 3)
    back = {}
    for k in (2, 3, 1):
        attn, part, *sums = main(k, visible, lengths, received[k], grads, caches, (attn, *sums[:2]))
        with jax.named_scope("return_query_grads"):
            back[k] = partner(part, k)
    near0, near1, near2, near3, *own_grads = sums[2:]
    with jax.named_scope("sum_prompt_grads_near"):
        near = [near0] + [partner(piece, 4 * j, "seq") for j, piece in ((1, near1), (2, near2), (3, near3))]
        partial = sum(piece.astype(jnp.float32) for piece in near)
    with jax.named_scope("return_kv_grads"):
        kv_back = [own_grads[0], back[1], partner(own_grads[1], 2), partner(own_grads[2], 3)]
    with jax.named_scope("sum_prompt_grads_far"):
        def block(index):
            return lax.dynamic_index_in_dim(partial, index, 0, keepdims=False)

        far = [block(high)] + [partner(block(high ^ j).astype(jnp.bfloat16), 16 * j, "seq") for j in (1, 2, 3)]
        query_grad = assemble(3, back[3], assemble(2, back[2], query_grad))
        far = after(far, kv_back[2], kv_back[3], query_grad)
        summed = sum(piece.astype(jnp.float32) for piece in far).astype(jnp.bfloat16)
    query_grad = assemble(1, back[1], query_grad)
    key_grad, value_grad = assemble_kv(kv_back)
    return (
        attn.reshape(1, 4 * rows, q_cols),
        query_grad[None],
        key_grad[None],
        value_grad[None],
        summed[:, :kv_cols],
        summed[:, kv_cols:],
    )


def solution(mesh):
    in_specs = (
        P("seq", "head", None),
        P("seq", "head", None),
        P("seq", "head", None),
        P("seq", None, "head"),
        P("seq"),
        P("seq", None),
        P("seq", "head"),
        P("seq", "head"),
    )
    out_specs = (
        P("seq", None, "head"),
        P("seq", "head", None),
        P("seq", "head", None),
        P("seq", "head", None),
        P("seq", "head"),
        P("seq", "head"),
    )
    return jax.shard_map(per_device, mesh=mesh, in_specs=in_specs, out_specs=out_specs, check_vma=False)
```

```python
import functools

import jax
import jax.numpy as jnp
from jax import lax
from jax.experimental import pallas as pl
from jax.experimental.pallas import tpu as pltpu
from jax.sharding import PartitionSpec as P

HD = 128
BLOCK = 128
GROUPS = 4
SCALE = HD ** (-0.5)
EXP_SCALE = SCALE * 1.4426950408889634
MASKED = -1e30
LAST = 3
VMEM_BYTES = 28 * 1024 * 1024
SMEM = pl.BlockSpec(memory_space=pltpu.SMEM)
VMEM = pl.BlockSpec(memory_space=pltpu.VMEM)
HBM = pl.BlockSpec(memory_space=pl.ANY)
PARAMS = pltpu.CompilerParams(vmem_limit_bytes=VMEM_BYTES)
SMALL_PARAMS = pltpu.CompilerParams(vmem_limit_bytes=16 * 1024 * 1024)


def dot_nt(left, right):
    return lax.dot_general(left, right, (((1,), (1,)), ((), ())), preferred_element_type=jnp.float32)


def dot_nn(left, right):
    return jnp.dot(left, right, preferred_element_type=jnp.float32)


def here():
    rank = lax.axis_index("seq") // GROUPS
    return lax.axis_index("head"), rank // 4, rank % 4


def prep_kernel(rows, visible_ref, p0, p1, p2, p3, own0, own1, own2, own3, kc, vc, kct, vct, own_rows, block_rows):
    me, high, low = here()
    own_rows[4 * rows :, :] = jnp.zeros((4 * BLOCK - 4 * rows, 4 * HD), jnp.float32)
    for k, ref in enumerate((own0, own1, own2, own3)):
        start = pl.multiple_of((me ^ k) * rows, 8)
        own_rows[pl.ds(start, rows), :] = ref[...].astype(jnp.float32)
    targets = ((kc, kct, 0), (kc, kct, 1), (vc, vct, 0), (vc, vct, 1))

    def place(slot, block):
        at = pl.multiple_of(slot * BLOCK, BLOCK)
        for part, (plain, turned, g) in enumerate(targets):
            piece = block[:, part * HD : (part + 1) * HD]
            plain[g, pl.ds(at, BLOCK), :] = piece.astype(jnp.bfloat16)
            turned[g, :, pl.ds(at, BLOCK)] = piece.T.astype(jnp.bfloat16)

    slot = jnp.int32(0)
    for b in range(4):
        seen = visible_ref[0, b]

        @pl.when(seen == 1)
        def _(b=b, slot=slot):
            for j, ref in enumerate((p0, p1, p2, p3)):
                start = pl.multiple_of((low ^ j) * 32, 32)
                block_rows[pl.ds(start, 32), :] = ref[high ^ b].astype(jnp.float32)
            place(slot, block_rows[...])

        slot = slot + seen
    for b in range(4):
        place(slot + b, own_rows[b * BLOCK : (b + 1) * BLOCK, :])

    @pl.when(slot < 4)
    def _():
        place(slot + 4, jnp.zeros((BLOCK, 4 * HD), jnp.float32))


def prep(visible, prompts, owns):
    rows = owns[0].shape[0]
    shapes = [(2, 8 * BLOCK, HD)] * 2 + [(2, HD, 8 * BLOCK)] * 2
    return pl.pallas_call(
        functools.partial(prep_kernel, rows),
        out_shape=[jax.ShapeDtypeStruct(shape, jnp.bfloat16) for shape in shapes],
        in_specs=[SMEM] + [VMEM] * 8,
        out_specs=[VMEM] * 4,
        scratch_shapes=[pltpu.VMEM((4 * BLOCK, 4 * HD), jnp.float32), pltpu.VMEM((BLOCK, 4 * HD), jnp.float32)],
        compiler_params=SMALL_PARAMS,
        name="prep",
    )(visible, *prompts, *owns)


def unit(n, heads, rows, position, seen, live, i, q_ref, g_ref, kc, vc, kct, vct, out_ref, qg_ref, dk_ref, dv_ref):
    keys = n * BLOCK
    kv = i // (8 // heads)
    pad = jnp.zeros((BLOCK - rows, HD), jnp.float32)
    row_live = lax.broadcasted_iota(jnp.int32, (rows, HD), 0) < live
    masked_blocks = min(3, n)
    first = keys - masked_blocks * BLOCK
    last = n - 1 - seen

    def at(h):
        return pl.ds(pl.multiple_of((i * heads + h) * HD, HD), HD)

    def padded(x):
        return jnp.concatenate([x, pad], axis=0).astype(jnp.bfloat16)

    def load_q(hs):
        return jnp.concatenate([padded(q_ref[:, at(h)].astype(jnp.float32)) for h in hs], axis=0)

    def load_g(hs):
        return jnp.concatenate(
            [padded(jnp.where(row_live, g_ref[:, at(h)].astype(jnp.float32), 0.0)) for h in hs], axis=0
        )

    def softmax(scores):
        shape = (BLOCK, scores.shape[1])
        s_at = lax.broadcasted_iota(jnp.int32, shape, 0)
        t_at = position * rows + lax.broadcasted_iota(jnp.int32, shape, 1) % BLOCK
        pieces = [scores[:first]] if first else []
        for j in range(masked_blocks):
            own = last - masked_blocks + 1 + j
            base = jnp.where(own >= 0, own * BLOCK, -100000)
            part = scores[first + j * BLOCK : first + (j + 1) * BLOCK]
            pieces.append(jnp.where(s_at + base <= t_at, part, MASKED))
        scores = jnp.concatenate(pieces, axis=0)
        top = jnp.max(scores, axis=0, keepdims=True)
        weights = jnp.exp2((scores - top) * EXP_SCALE)
        return weights * (1.0 / jnp.sum(weights, axis=0, keepdims=True))

    def dscore_of(weights, dprob):
        product = weights * dprob
        delta = jnp.sum(product, axis=0, keepdims=True)
        return (product - weights * delta).astype(jnp.bfloat16)

    def store(hs, mixed, query_grad):
        for j, h in enumerate(hs):
            lanes = slice(j * BLOCK, (j + 1) * BLOCK)
            mixed_rows = mixed[:, lanes].T.astype(jnp.float32)[:rows]
            out_ref[:, at(h)] = jnp.where(row_live, mixed_rows, 0.0).astype(jnp.bfloat16)
            qg_ref[:, at(h)] = query_grad[:, lanes].T[:rows]

    key, value, key_t, value_t = kc[kv, :keys, :], vc[kv, :keys, :], kct[kv, :, :keys], vct[kv, :, :keys]

    half = heads // 2
    ha, hb = list(range(half)), list(range(half, heads))
    qa, ga = load_q(ha), load_g(ha)
    sa = dot_nt(key, qa)
    qb, gb = load_q(hb), load_g(hb)
    sb = dot_nt(key, qb)
    wa = softmax(sa)
    la = wa.astype(jnp.bfloat16)
    pa = dot_nt(value, ga)
    wb = softmax(sb)
    lb = wb.astype(jnp.bfloat16)
    pb = dot_nt(value, gb)
    ma = dot_nn(value_t, la).astype(jnp.bfloat16)
    da = dscore_of(wa, pa)
    mb = dot_nn(value_t, lb).astype(jnp.bfloat16)
    db = dscore_of(wb, pb)
    xa = (dot_nn(key_t, da) * SCALE).astype(jnp.bfloat16)
    dv_ref[kv, :keys, :] += dot_nn(jnp.concatenate([la, lb], axis=1), jnp.concatenate([ga, gb], axis=0))
    xb = (dot_nn(key_t, db) * SCALE).astype(jnp.bfloat16)
    dk_ref[kv, :keys, :] += dot_nn(jnp.concatenate([da, db], axis=1), jnp.concatenate([qa, qb], axis=0))
    store(ha, ma, xa)
    store(hb, mb, xb)


def finish(rows, visible_ref, dk_ref, dv_ref, pieces, owns):
    me, _, low = here()
    parts = ((dk_ref, 0, SCALE), (dk_ref, 1, SCALE), (dv_ref, 0, 1.0), (dv_ref, 1, 1.0))
    slot = jnp.int32(0)
    for b in range(4):
        seen = visible_ref[0, b]

        @pl.when(seen == 1)
        def _(b=b, slot=slot):
            for j, piece in enumerate(pieces):
                source = pl.ds(pl.multiple_of(slot * BLOCK + (low ^ j) * 32, 32), 32)
                for part, (ref, g, scale) in enumerate(parts):
                    piece[b, :, part * HD : (part + 1) * HD] = (ref[g, source, :] * scale).astype(piece.dtype)

        @pl.when(seen != 1)
        def _(b=b):
            for piece in pieces:
                piece[b] = jnp.zeros(piece.shape[1:], piece.dtype)

        slot = slot + seen
    for k, own in enumerate(owns):
        source = pl.ds(pl.multiple_of(slot * BLOCK + (me ^ k) * rows, 8), rows)
        for part, (ref, g, scale) in enumerate(parts):
            own[:, own.shape[1] - (4 - part) * HD : own.shape[1] - (3 - part) * HD] = (ref[g, source, :] * scale).astype(own.dtype)


def main_kernel(k, heads, rows, visible_ref, length_ref, q_ref, kc, vc, kct, vct, grads, *rest):
    if k == 0:
        attn, wide, dk_ref, dv_ref, g_ref, out_ref, sems, qg_ref = rest
        dk_ref[...] = jnp.zeros_like(dk_ref)
        dv_ref[...] = jnp.zeros_like(dv_ref)
    else:
        _, _, _, attn, qg_ref, dk_ref, dv_ref, *finals, g_ref, out_ref, sems = rest
    me = lax.axis_index("head")
    position = me ^ k
    seen = visible_ref[0, 0] + visible_ref[0, 1] + visible_ref[0, 2] + visible_ref[0, 3]
    live = length_ref[0] - position * rows
    cols = q_ref.shape[1]
    size = heads * HD
    steps = cols // size

    def chunk(i):
        return pl.ds(pl.multiple_of(i * size, size), size)

    def grad_copy(i):
        return pltpu.make_async_copy(grads.at[position, :, chunk(i)], g_ref.at[:, chunk(i)], sems.at[0, i])

    def out_copies(i):
        copies = [pltpu.make_async_copy(out_ref.at[:, chunk(i)], attn.at[position, :, chunk(i)], sems.at[1, i])]
        if k == 0:
            target = wide.at[:, pl.ds(pl.multiple_of(me * cols + i * size, size), size)]
            copies.append(pltpu.make_async_copy(qg_ref.at[:, chunk(i)], target, sems.at[2, i]))
        return copies

    def send(i):
        for copy in out_copies(i):
            copy.start()

    @pl.when(live <= 0)
    def _():
        out_ref[...] = jnp.zeros_like(out_ref)
        qg_ref[:, :cols] = jnp.zeros((rows, cols), jnp.bfloat16)
        for i in range(steps):
            send(i)

    @pl.when(live > 0)
    def _():
        for i in range(steps):
            grad_copy(i).start()

    count = jnp.where(live > 0, (seen + position + 2) // 2 * 2, 0)
    for n in (2, 4, 6, 8):

        @pl.when(count == n)
        def _(n=n):
            @pl.loop(0, steps)
            def _(i):
                grad_copy(i).wait()
                unit(n, heads, rows, position, seen, live, i, q_ref, g_ref, kc, vc, kct, vct, out_ref, qg_ref, dk_ref, dv_ref)
                send(i)

    if k == LAST:
        finish(rows, visible_ref, dk_ref, dv_ref, finals[:4], [*finals[4:], qg_ref])
    for i in range(steps):
        for copy in out_copies(i):
            copy.wait()


def main(k, visible, lengths, q, grad, caches, carried, heads=4):
    rows, cols = q.shape
    total = jax.ShapeDtypeStruct((2, 8 * BLOCK, HD), jnp.float32)
    small = jax.ShapeDtypeStruct((rows, cols), jnp.bfloat16)
    wide = jax.ShapeDtypeStruct((rows, 4 * cols), jnp.bfloat16)
    attn = jax.ShapeDtypeStruct(grad.shape, jnp.bfloat16)
    buffer = pltpu.VMEM((rows, cols), jnp.bfloat16)
    first = k == 0
    finals = []
    if k == LAST:
        kv = 4 * HD
        small = jax.ShapeDtypeStruct((rows, cols + kv), jnp.bfloat16)
        finals = [jax.ShapeDtypeStruct((4, 32, kv), jnp.bfloat16 if j else jnp.float32) for j in range(4)]
        finals += [jax.ShapeDtypeStruct((rows, kv), jnp.bfloat16)] * 3
    flops = 6 * 2 * 16 * rows * 800 * HD
    return pl.pallas_call(
        functools.partial(main_kernel, k, heads, rows),
        out_shape=[attn, wide if first else small, total, total] + finals,
        in_specs=[SMEM] * 2 + [VMEM] * 5 + [HBM] + ([] if first else [HBM, VMEM, VMEM]),
        out_specs=[HBM, HBM if first else VMEM, VMEM, VMEM] + [VMEM] * len(finals),
        scratch_shapes=[buffer] * 2 + [pltpu.SemaphoreType.DMA((3, cols // (heads * HD)))] + [buffer] * first,
        input_output_aliases={} if first else {8: 0, 9: 2, 10: 3},
        compiler_params=PARAMS,
        cost_estimate=pl.CostEstimate(flops=flops, bytes_accessed=6000000, transcendentals=0),
        name="rows_%d" % k,
    )(visible, lengths, q, *caches, grad, *([] if first else carried))


def run_all(copies):
    for copy in copies:
        copy.start()
    for copy in copies:
        copy.wait()


def assemble_kernel(ks, *refs):
    pieces, wide, sems = refs[: len(ks)], refs[len(ks) + 1], refs[len(ks) + 2]
    cols = wide.shape[1] // 4
    copies = []
    for j, (k, piece) in enumerate(zip(ks, pieces)):
        at = pl.ds(pl.multiple_of((lax.axis_index("head") ^ k) * cols, cols), cols)
        copies.append(pltpu.make_async_copy(piece, wide.at[:, at], sems.at[j]))
    run_all(copies)


def assemble(ks, pieces, wide):
    return pl.pallas_call(
        functools.partial(assemble_kernel, ks),
        out_shape=jax.ShapeDtypeStruct(wide.shape, wide.dtype),
        in_specs=[VMEM] * len(ks) + [HBM],
        out_specs=HBM,
        scratch_shapes=[pltpu.SemaphoreType.DMA((len(ks),))],
        input_output_aliases={len(ks): 0},
        compiler_params=SMALL_PARAMS,
        name="assemble",
    )(*pieces, wide)


def assemble_last_kernel(p0, p1, p2, p3, _, wide, key_grad, value_grad, sems):
    me = lax.axis_index("head")
    cols = p0.shape[1] // 2
    q_cols = wide.shape[1] // 4
    at = pl.ds(pl.multiple_of((me ^ LAST) * q_cols, q_cols), q_cols)
    copies = [pltpu.make_async_copy(p3.at[:, :q_cols], wide.at[:, at], sems.at[2, 0])]
    for k, piece in enumerate((p0, p1, p2, p3)):
        at = pl.ds(pl.multiple_of((me ^ k) * cols, cols), cols)
        offset = piece.shape[1] - 2 * cols
        for j, target in enumerate((key_grad, value_grad)):
            source = piece.at[:, offset + j * cols : offset + (j + 1) * cols]
            copies.append(pltpu.make_async_copy(source, target.at[:, at], sems.at[j, k]))
    run_all(copies)


def assemble_last(pieces, wide):
    rows, cols = pieces[0].shape
    shape = jax.ShapeDtypeStruct((rows, 2 * cols), pieces[0].dtype)
    return pl.pallas_call(
        assemble_last_kernel,
        out_shape=[jax.ShapeDtypeStruct(wide.shape, wide.dtype), shape, shape],
        in_specs=[VMEM] * 4 + [HBM],
        out_specs=[HBM] * 3,
        scratch_shapes=[pltpu.SemaphoreType.DMA((3, 4))],
        input_output_aliases={4: 0},
        compiler_params=SMALL_PARAMS,
        name="assemble_last",
    )(*pieces, wide)


def partner(value, mask, axis="head"):
    pairs = [(source, source ^ mask) for source in range(lax.axis_size(axis))]
    return lax.ppermute(value, axis, pairs)


def after(value, *earlier):
    return lax.optimization_barrier((value, *earlier))[0]


def per_device(query_roll, key_roll, value_roll, out_grad, lengths, visible, key_prompt, value_prompt):
    rows = query_roll.shape[1]
    me, high, low = here()
    queries, keys, values = query_roll[0], key_roll[0], value_roll[0]
    q_cols = queries.shape[1] // 4
    kv_cols = keys.shape[1] // 4

    def columns(array, index, size):
        return lax.dynamic_slice_in_dim(array, index * size, size, 1)

    def kv_piece(index):
        return jnp.concatenate([columns(keys, index, kv_cols), columns(values, index, kv_cols)], axis=1)

    with jax.named_scope("gather_prompt_far"):
        mine = jnp.concatenate([key_prompt, value_prompt], axis=1)
        four = jnp.stack([mine] + [partner(mine, 16 * j, "seq") for j in (1, 2, 3)])
    with jax.named_scope("gather_prompt_near"):
        prompts = [four] + [partner(four, 4 * j, "seq") for j in (1, 2, 3)]
    with jax.named_scope("send_kv"):
        owns = [kv_piece(me), None] + [partner(kv_piece(me ^ k), k) for k in (2, 3)]
        owns[1] = partner(after(kv_piece(me ^ 1), prompts[1]), 1)
    caches = prep(visible, prompts, owns)
    grads = out_grad.reshape(4, rows, out_grad.shape[2])
    q_pieces = [columns(queries, me ^ k, q_cols) for k in range(4)]
    with jax.named_scope("send_queries"):
        early = after(q_pieces[1:3], *prompts)
        received = {k: partner(early[k - 1], k) for k in (1, 2)}
    attn, query_grad, *sums = main(0, visible, lengths, q_pieces[0], grads, caches, None)
    with jax.named_scope("send_queries"):
        received[3] = partner(after(q_pieces[3], sums[0]), 3)
    back = {}
    for k in (2, 1, 3):
        sums = after(sums, received[3]) if k == 1 else after(sums, back[2]) if k == 3 else sums
        attn, part, *sums = main(k, visible, lengths, received[k], grads, caches, (attn, *sums[:2]))
        with jax.named_scope("return_query_grads"):
            back[k] = partner(part, k)
    near0, near1, near2, near3, *own_grads = after(sums[2:], back[1])
    with jax.named_scope("sum_prompt_grads_near"):
        near = [near0] + [partner(piece, 4 * j, "seq") for j, piece in ((1, near1), (2, near2), (3, near3))]
        partial = sum(piece.astype(jnp.float32) for piece in near)
    with jax.named_scope("return_kv_grads"):
        kv_back = [own_grads[0], partner(own_grads[1], 1), partner(own_grads[2], 2), back[3]]
    with jax.named_scope("sum_prompt_grads_far"):
        def block(index):
            return lax.dynamic_index_in_dim(partial, index, 0, keepdims=False)

        far = [block(high)] + [partner(block(high ^ j).astype(jnp.bfloat16), 16 * j, "seq") for j in (1, 2, 3)]
        query_grad = assemble((1, 2), (back[1], back[2]), query_grad)
        query_grad, key_grad, value_grad = assemble_last(kv_back, query_grad)
        far = after(far, query_grad)
        summed = sum(piece.astype(jnp.float32) for piece in far).astype(jnp.bfloat16)
    return (
        attn.reshape(1, 4 * rows, q_cols),
        query_grad[None],
        key_grad[None],
        value_grad[None],
        summed[:, :kv_cols],
        summed[:, kv_cols:],
    )


def solution(mesh):
    in_specs = (
        P("seq", "head", None),
        P("seq", "head", None),
        P("seq", "head", None),
        P("seq", None, "head"),
        P("seq"),
        P("seq", None),
        P("seq", "head"),
        P("seq", "head"),
    )
    out_specs = (
        P("seq", None, "head"),
        P("seq", "head", None),
        P("seq", "head", None),
        P("seq", "head", None),
        P("seq", "head"),
        P("seq", "head"),
    )
    return jax.shard_map(per_device, mesh=mesh, in_specs=in_specs, out_specs=out_specs, check_vma=False)
```
